128 devices in a mesh: corpus: 32 (over z, x, core), replica: 4 (over y).
Axes of the slice: x: 4, y: 4, z: 4, core: 2. Of those that a mesh axis runs over, the one named last changes fastest.
Arguments:
- queries: bfloat16 [1024, 32, 128], P(('corpus', 'replica')), may hold values from -0.5390625 to 0.5390625
- cand_dev: int32 [1024, 16], P(('corpus', 'replica')), may hold values from 0 to 127, all different within a row; in each aligned block of 8 rows (0 to 7, 8 to 15, ...) at most 2 rows name the same one
- cand_slot: int32 [1024, 256], P(('corpus', 'replica')), may hold values from 0 to 511
- codes: int32 [65536, 4096], P(('corpus', 'replica')), may hold values from 0 to 255
- cent_ids: int32 [65536, 128], P(('corpus', 'replica')), may hold values from 0 to 65535
- lengths: int32 [65536], P(('corpus', 'replica')), may hold values from 1 to 128
- centroids: bfloat16 [65536, 128], replicated, may hold values from -0.5390625 to 0.5390625
- buckets: float32 [4], replicated, may hold values from -0.36 to 0.36
Outputs:
- scores: float32 [1024, 256], P(('corpus', 'replica'))
The draws below stay inside these ranges and needn't reach their ends.
Inputs may be any that keep to these rules, and one draw needn't show every extreme that they name: `cand_dev`: each row names 16 different devices. Among the 8 rows of one device, no device is named more than 2 times, and some device is named exactly 2 times in some or all of these blocks.
All inputs are finite; a program needn't handle non-finite values.
Results may differ from the reference program's by a relative error of at most 0.0003.
Values may be sent and summed in bfloat16 or wider, within the bound.
No kernel may reach another device: no remote copies, remote signals or barrier semaphores. Data moves between devices by JAX's collectives and lax.ppermute only.
A program may use at most 256 MiB of HBM per device.

```python
import math
import jax
import jax.numpy as jnp
import numpy as np
from jax import lax

DIM = 128
QTOK = 32
PTOK = 128
NCENT = 65536
TOPDEV = 16
PER = 16
Q_DEV = 8
PASS_DEV = 512
WORDS = 32
QCAP = 2
QUERIES = 1024
PASSAGES = 65536
DEVICES = 128


def with_ends(array, own_key, smallest, high):
    extent = array.shape
    spot = [jax.random.randint(jax.random.fold_in(own_key, axis), (), 0, extent[axis]) for axis in range(len(extent))]
    array = array.at[tuple(spot)].set(smallest)
    longest = extent.index(max(extent))
    spot[longest] = (spot[longest] + 1) % extent[longest]
    return array.at[tuple(spot)].set(high)


def level_of(own_key, shape, split, least, top_value):
    gain = 1.0
    for position, shards_of in split:
        heights = jax.random.uniform(jax.random.fold_in(jax.random.fold_in(own_key, 6), position), (shards_of,), jnp.float32, least / len(split), top_value / len(split))
        gain = gain * jnp.repeat(jnp.exp(heights), shape[position] // shards_of).reshape((-1,) + (1,) * (len(shape) - 1 - position))
    return gain


def deal_out(key, own, number, rows, amount, top, limit, skew):
    ranking = jax.random.permutation(key, amount)
    heavy_load, usual = portions_of(amount, rows * top, limit, skew, True), portions_of(amount, rows * top, limit, skew, False)
    places = jnp.arange(amount)

    def named(sizes, turn):
        used = int((sizes > 0).sum())
        fixed = max(1, used // 4)
        passed = fixed + (places - fixed + turn * (used - fixed)) % max(1, amount - fixed)
        return jnp.zeros((amount,), jnp.int32).at[ranking[jnp.where(places < fixed, places, passed)]].set(jnp.asarray(sizes, jnp.int32))

    sizes = jnp.where(number % 4 == 0, named(heavy_load, number // 4), named(usual, number - number // 4 - 1))
    mixed = jax.random.permutation(jax.random.fold_in(own, 3), amount)
    source_of, receiver = mixed[0:amount // 2 * 2:2], mixed[1:amount // 2 * 2:2]
    room = jnp.minimum(sizes[source_of] - 1, limit - sizes[receiver]) // 2
    room = jnp.where((source_of == ranking[0]) | (receiver == ranking[0]) | (sizes[receiver] == 0), 0, jnp.maximum(room, 0))
    passed = jax.random.randint(jax.random.fold_in(own, 4), (amount // 2,), 0, 1 << 20) % (room + 1)
    sizes = sizes.at[source_of].add(-passed).at[receiver].add(passed)
    items = jnp.searchsorted(jnp.cumsum(sizes), jnp.arange(rows * top), side="right").astype(jnp.int32)
    listing = items.reshape(top, rows).T
    listing = listing[jax.random.permutation(jax.random.fold_in(own, 1), rows)]
    turn = jax.random.randint(jax.random.fold_in(own, 2), (rows, 1), 0, top)
    return jnp.take_along_axis(listing, (jnp.arange(top)[None, :] + turn) % top, axis=1)


def portions_of(amount, total, limit, skew, full):
    portions = [(1 << 20) // math.isqrt(grade ** skew) + 1 for grade in range(1, amount + 1)]
    largest = limit if full else min(limit, max(-(-total // amount), total * portions[0] // sum(portions)))
    least = 1 if total - largest >= amount - 1 else 0
    given, surplus = [largest] + [least] * (amount - 1), total - largest - least * (amount - 1)
    while surplus > 0:
        candidates = [i for i in range(1, amount) if given[i] < largest] or [i for i in range(1, amount) if given[i] < limit]
        whole, budget = sum([portions[i] for i in candidates]), surplus
        for i in candidates:
            addition = min(limit - given[i], max(1, budget * portions[i] // whole), surplus)
            given[i] = given[i] + addition
            surplus = surplus - addition
    return np.array(given)


def bell_draw(stream_key, dims, deviation, bound, shards=(), held_as=jnp.bfloat16):
    drawn = jax.random.normal(stream_key, dims, jnp.float32) * deviation
    if len(shards) > 0:
        drawn = level_of(stream_key, dims, shards, -0.22, 0.18) * drawn
    return jnp.clip(drawn, min=-bound, max=bound).astype(held_as)


def setup_inputs(seed: int = 0) -> dict:
    arg_keys = jax.random.split(jax.random.key(seed), 9)
    queries = bell_draw(arg_keys[0], (QUERIES, QTOK, DIM), 0.09, 0.5390625, ((0, 128),))
    cand_dev_keys = jax.random.split(jax.random.fold_in(arg_keys[1], 1), QUERIES // Q_DEV)
    cand_dev_turns = jax.random.permutation(jax.random.fold_in(arg_keys[1], 3), QUERIES // Q_DEV)
    cand_dev = jax.vmap(lambda own, number: deal_out(jax.random.fold_in(arg_keys[1], 2), own, number, Q_DEV, DEVICES, TOPDEV, QCAP, 2))(cand_dev_keys, cand_dev_turns).reshape((QUERIES, TOPDEV))
    cand_slot = with_ends(jax.random.randint(arg_keys[2], (QUERIES, TOPDEV * PER), 0, PASS_DEV), jax.random.fold_in(arg_keys[2], 1), 0, PASS_DEV - 1).astype(jnp.int32)
    codes = with_ends(jax.random.randint(arg_keys[3], (PASSAGES, PTOK * WORDS), 0, 256), jax.random.fold_in(arg_keys[3], 1), 0, 255).astype(jnp.int32)
    cent_ids = with_ends(jax.random.randint(arg_keys[4], (PASSAGES, PTOK), 0, NCENT), jax.random.fold_in(arg_keys[4], 1), 0, NCENT - 1).astype(jnp.int32)
    lengths = with_ends(jax.random.randint(arg_keys[5], (PASSAGES,), 1, PTOK + 1), jax.random.fold_in(arg_keys[5], 1), 1, PTOK).astype(jnp.int32)
    centroids = bell_draw(arg_keys[6], (NCENT, DIM), 0.09, 0.5390625)
    buckets = bell_draw(arg_keys[7], (4,), 0.06, 0.36, (), jnp.float32)
    return {"queries": queries, "cand_dev": cand_dev, "cand_slot": cand_slot, "codes": codes, "cent_ids": cent_ids, "lengths": lengths, "centroids": centroids, "buckets": buckets}


def unpack(code_rows, cid_rows, centroids, buckets):
    words = code_rows.reshape(code_rows.shape[:-1] + (PTOK, DIM // 4))
    shifts = 2 * jnp.arange(4, dtype=jnp.int32)
    bits = jnp.bitwise_and(jnp.right_shift(words[..., None], shifts), 3)
    bits = bits.reshape(words.shape[:-1] + (DIM,))
    residual = jnp.where(bits == 0, buckets[0], jnp.where(bits == 1, buckets[1], jnp.where(bits == 2, buckets[2], buckets[3])))
    embed = centroids[cid_rows].astype(jnp.float32) + residual
    embed = embed * lax.rsqrt(lax.optimization_barrier(jnp.sum(embed * embed, axis=-1, keepdims=True)) + 1e-06)
    return embed.astype(jnp.bfloat16)

def reference(queries, cand_dev, cand_slot, codes, cent_ids, lengths, centroids, buckets):

    def one_query(items):
        query_row, devices_row, slots_row = items
        rows = (devices_row[:, None] * PASS_DEV + slots_row.reshape(TOPDEV, PER)).reshape(-1).astype(jnp.int32)
        embed = unpack(codes[rows], cent_ids[rows], centroids, buckets)
        sims = jnp.einsum('qf,ptf->qpt', query_row.astype(jnp.float32), embed.astype(jnp.float32))
        live = jnp.arange(PTOK, dtype=jnp.int32)[None, :] < lengths[rows][:, None]
        best = lax.optimization_barrier(jnp.max(jnp.where(live[None], sims, -1e+30), axis=2))
        return lax.optimization_barrier(jnp.sum(best, axis=0))
    return lax.map(one_query, (queries, cand_dev, cand_slot))
```

```python
import functools

import jax
import jax.numpy as jnp
from jax import lax
from jax.experimental import pallas as pl
from jax.experimental.pallas import tpu as pltpu
from jax.sharding import PartitionSpec as P

DIM = 128
PTOK = 128
CHUNK = 32
AXES = ("corpus", "replica")

TAB_STEP = 1024
TAB_BUFS = 10
GROUP_BITS = 3
GROUP = 1 << GROUP_BITS
PARTS = 8


def load_table(cent, tab, buf, sem):
    steps = cent.shape[0] // TAB_STEP

    def copy(i, slot):
        start = pl.multiple_of(i * TAB_STEP, TAB_STEP)
        return pltpu.make_async_copy(cent.at[pl.ds(start, TAB_STEP)], buf.at[slot], sem.at[slot])

    for i in range(min(TAB_BUFS - 1, steps)):
        copy(i, i).start()

    def body(i, carry):
        @pl.when(i + TAB_BUFS - 1 < steps)
        def _():
            copy(i + TAB_BUFS - 1, lax.rem(i + TAB_BUFS - 1, TAB_BUFS)).start()

        slot = lax.rem(i, TAB_BUFS)
        copy(i, slot).wait()
        start = pl.multiple_of(i * TAB_STEP, TAB_STEP)
        tab[pl.ds(start, TAB_STEP), :] = buf[slot].astype(jnp.float32)
        return carry

    lax.fori_loop(0, steps, body, 0)


def unpack_kernel(
    items, starts, lefts, lasts, bounds, buckets, ids_hbm, codes_hbm, cent, out,
    tab, buf, ids, codes, stored, centre, words, raws, squares, spread_of, ones,
    sem, ids_sem, codes_sem, out_sem,
):
    n_items = items.shape[0]
    parts = codes_sem.shape[0]
    code_rows = codes.shape[0] // parts
    part_chunks = n_items // parts

    def codes_copy(j):
        at = pl.ds(pl.multiple_of(j * code_rows, code_rows), code_rows)
        return pltpu.make_async_copy(codes_hbm.at[at], codes.at[at], codes_sem.at[j])

    def out_copy(j):
        at = pl.ds(j * part_chunks, part_chunks)
        return pltpu.make_async_copy(stored.at[at], out.at[at], out_sem)

    ids_copy = pltpu.make_async_copy(ids_hbm, ids, ids_sem)
    ids_copy.start()
    codes_copy(0).start()
    lane = lax.broadcasted_iota(jnp.int32, (8, DIM), 1)
    sub = lax.broadcasted_iota(jnp.int32, (8, DIM), 0)
    low_bit = jnp.left_shift(1, 2 * jnp.bitwise_and(lane, 3))
    high_bit = jnp.left_shift(2, 2 * jnp.bitwise_and(lane, 3))
    source = lax.broadcasted_iota(jnp.int32, (DIM, 4 * DIM), 0)
    target = jnp.right_shift(lax.broadcasted_iota(jnp.int32, (DIM, 4 * DIM), 1), 2)
    spread_of[...] = jnp.where(source == target, 1.0, 0.0).astype(jnp.bfloat16)
    ones[...] = jnp.ones_like(ones)
    centre[1] = jnp.zeros_like(centre[1])
    words[1] = jnp.zeros_like(words[1])
    raws[...] = jnp.zeros_like(raws)
    squares[...] = jnp.zeros_like(squares)
    load_table(cent, tab, buf, sem)
    for j in range(1, parts):
        codes_copy(j).start()
    ids_copy.wait()
    b0, b1, b2, b3 = (buckets[i] for i in range(4))

    def gather(group, side):
        code_rows = []
        for n in range(GROUP):
            item = group * GROUP + n
            code = items[item]
            code_rows.append(codes[pl.ds(starts[item], 8, stride=8), :])
            for k in range(4):
                for r in range(8):
                    token = ids.at[pl.ds((4 * r + k) * n_items, n_items)][code]
                    centre[side, pl.ds(CHUNK * n + 8 * k + r, 1), :] = tab[pl.ds(token, 1), :]
        packed = jnp.concatenate(code_rows, axis=0).astype(jnp.float32).astype(jnp.bfloat16)
        words[side] = jnp.dot(packed, spread_of[...], preferred_element_type=jnp.float32)

    def decode(side):
        for n in range(GROUP):
            parts = []
            for k in range(4):
                at = pl.ds(CHUNK * n + 8 * k, 8)
                word = words[side, pl.ds(8 * n, 8), pl.ds(DIM * k, DIM)].astype(jnp.int32)
                low = jnp.bitwise_and(word, low_bit) != 0
                high = jnp.bitwise_and(word, high_bit) != 0
                residual = jnp.where(high, jnp.where(low, b3, b2), jnp.where(low, b1, b0))
                raw = centre[side, at, :] + residual
                raws[side, at, :] = raw
                parts.append(raw * raw)
            for h in range(2):
                square = jnp.concatenate(parts[2 * h : 2 * h + 2], axis=0)
                top = square.astype(jnp.bfloat16)
                rest = (square - top.astype(jnp.float32)).astype(jnp.bfloat16)
                squares[side, pl.ds(CHUNK * n + 16 * h, 16), :] = jnp.concatenate([top, rest], axis=1)

    def finish(group, side):
        sums = jnp.dot(squares[side], ones[...], preferred_element_type=jnp.float32)
        for n in range(GROUP):
            item = group * GROUP + n
            left = lefts[item]
            embeds = []
            for k in range(4):
                at = CHUNK * n + 8 * k
                total = sums[at : at + 8, :]
                embeds.append(raws[side, pl.ds(at, 8), :] * lax.rsqrt(total + 1e-06))
            first = jnp.broadcast_to(embeds[0][0:1, :], (8, DIM))
            embeds = [jnp.where(4 * sub + k < left, embeds[k], first) for k in range(4)]
            stored[items[item]] = jnp.concatenate(embeds, axis=0).astype(jnp.bfloat16)

    def body(i, carry):
        for side in range(2):
            group = 2 * i + side
            finish(jnp.maximum(group - 2, 0), side)
            decode(1 - side)
            gather(jnp.minimum(group, n_items // GROUP - 1), side)
        return carry

    def repeat(p, carry):
        for q in range(4):
            begin = 4 * (4 * p + q)
            last = lasts[4 * p + q]
            for c in range(1, 4):
                stored[begin + c] = stored[jnp.minimum(begin + c, last)]
        return carry

    n_pass = lasts.shape[0]

    def close(j):
        per = n_pass // parts
        lax.fori_loop(j * (per // 4), (j + 1) * (per // 4), repeat, 0)
        out_copy(j).start()

    def part(j, begin):
        codes_copy(j).wait()
        lax.fori_loop(begin, bounds[j], body, 0)

        @pl.when(j > 0)
        def _():
            close(j - 1)

        return bounds[j]

    lax.fori_loop(0, parts, part, jnp.int32(0))
    close(parts - 1)
    for j in range(parts):
        out_copy(j).wait()


def plan_items(lengths, parts):
    n_pass = lengths.shape[0]
    chunks = jnp.right_shift(lengths + (CHUNK - 1), 5)
    ends = jnp.cumsum(chunks)
    order = jnp.minimum(jnp.arange(4 * n_pass, dtype=jnp.int32), ends[-1] - 1)
    passed = ends[None, :] <= order[:, None]
    which = jnp.sum(passed.astype(jnp.int32), axis=1)
    begin = jnp.max(jnp.where(passed, ends[None, :], 0), axis=1)
    length = jnp.sum(jnp.where(jnp.arange(n_pass)[None, :] == which[:, None], lengths[None, :], 0), axis=1)
    ch = order - begin
    items = 4 * which + ch
    starts = (jnp.right_shift(which, 3) * CHUNK + ch * 8) * 8 + jnp.bitwise_and(which, 7)
    lefts = length - CHUNK * ch
    lasts = 4 * jnp.arange(n_pass, dtype=jnp.int32) + chunks - 1
    per = n_pass // parts
    bounds = jnp.right_shift(ends[per - 1 :: per], GROUP_BITS + 1)
    groups = jnp.right_shift(ends[-1] + (GROUP - 1), GROUP_BITS)
    bounds = jnp.where(jnp.arange(parts) == parts - 1, jnp.right_shift(groups + 3, 1), bounds)
    return items, starts, lefts, lasts, bounds


def unpack(ids, lengths, buckets, codes, centroids):
    n_pass = codes.shape[0]
    n_items = 4 * n_pass
    plan = plan_items(lengths, PARTS)
    tiles = codes.reshape(n_pass // 8, 8, CHUNK, DIM).transpose(0, 2, 1, 3).reshape(-1, DIM)
    by_place = ids.reshape(n_items, CHUNK).T.reshape(-1)
    smem = pl.BlockSpec(memory_space=pltpu.SMEM)
    anywhere = pl.BlockSpec(memory_space=pl.ANY)
    rows = GROUP * CHUNK
    return pl.pallas_call(
        unpack_kernel,
        in_specs=[smem] * 6 + [anywhere] * 3,
        out_specs=anywhere,
        out_shape=jax.ShapeDtypeStruct((n_items, CHUNK, DIM), jnp.bfloat16),
        scratch_shapes=[
            pltpu.VMEM(centroids.shape, jnp.float32),
            pltpu.VMEM((TAB_BUFS, TAB_STEP, DIM), jnp.bfloat16),
            pltpu.SMEM((n_pass * PTOK,), jnp.int32),
            pltpu.VMEM(tiles.shape, jnp.int32),
            pltpu.VMEM((n_items, CHUNK, DIM), jnp.bfloat16),
            pltpu.VMEM((2, rows, DIM), jnp.float32),
            pltpu.VMEM((2, 8 * GROUP, 4 * DIM), jnp.float32),
            pltpu.VMEM((2, rows, DIM), jnp.float32),
            pltpu.VMEM((2, rows, 2 * DIM), jnp.bfloat16),
            pltpu.VMEM((DIM, 4 * DIM), jnp.bfloat16),
            pltpu.VMEM((2 * DIM, DIM), jnp.bfloat16),
            pltpu.SemaphoreType.DMA((TAB_BUFS,)),
            pltpu.SemaphoreType.DMA,
            pltpu.SemaphoreType.DMA((PARTS,)),
            pltpu.SemaphoreType.DMA,
        ],
        compiler_params=pltpu.CompilerParams(vmem_limit_bytes=60 * 2**20),
        cost_estimate=pl.CostEstimate(flops=10**9, bytes_accessed=40 * 2**20, transcendentals=0),
        name="unpack",
    )(*plan, buckets, by_place, tiles, centroids)


def score_kernel(rows_per, slots, recv, stored_hbm, out, stored, best, sem):
    parts = sem.shape[0]
    size = stored.shape[0] // parts

    def copy(i):
        return pltpu.make_async_copy(
            stored_hbm.at[pl.ds(i * size, size)], stored.at[pl.ds(i * size, size)], sem.at[i]
        )

    for i in range(parts):
        copy(i).start()
    for i in range(parts):
        copy(i).wait()

    def one(src, which):
        q = recv[pl.ds(pl.multiple_of(src * rows_per + 32 * which, 16), 32), :]
        zero = jnp.zeros_like(q)
        pair_q = jnp.concatenate(
            [jnp.concatenate([q, zero], axis=1), jnp.concatenate([zero, q], axis=1)], axis=0
        )
        query = 2 * src + which
        sides = [[], []]
        for place in range(16):
            sides[place % 2].append(stored[slots[query * 16 + place]])
        both = jnp.concatenate([jnp.concatenate(side, axis=0) for side in sides], axis=1)
        sims = lax.dot_general(
            both, pair_q, (((1,), (1,)), ((), ())), preferred_element_type=jnp.float32
        )
        tops = [
            jnp.max(sims[PTOK * pair : PTOK * (pair + 1), :], axis=0, keepdims=True)
            for pair in range(8)
        ]
        best[pl.ds(query, 1), :] = jnp.concatenate(tops, axis=1)

    def body(src, carry):
        one(src, 0)
        one(src, 1)
        return carry

    lax.fori_loop(0, recv.shape[0] // rows_per, body, 0)
    width = best.shape[1]
    member = lax.broadcasted_iota(jnp.int32, (width, 16), 0) // 32
    member = member == lax.broadcasted_iota(jnp.int32, (width, 16), 1)
    out[...] = jnp.dot(
        best[...],
        member.astype(jnp.float32),
        precision=lax.Precision.HIGHEST,
        preferred_element_type=jnp.float32,
    )


def score(rows_per, slots, recv, stored):
    devices = recv.shape[0] // rows_per
    return pl.pallas_call(
        functools.partial(score_kernel, rows_per),
        in_specs=[
            pl.BlockSpec(memory_space=pltpu.SMEM),
            pl.BlockSpec(memory_space=pltpu.VMEM),
            pl.BlockSpec(memory_space=pl.ANY),
        ],
        out_specs=pl.BlockSpec(memory_space=pltpu.VMEM),
        out_shape=jax.ShapeDtypeStruct((2 * devices, 16), jnp.float32),
        scratch_shapes=[
            pltpu.VMEM((stored.size // (PTOK * DIM), PTOK, DIM), jnp.bfloat16),
            pltpu.VMEM((2 * devices, 16 * 32), jnp.float32),
            pltpu.SemaphoreType.DMA((16,)),
        ],
        compiler_params=pltpu.CompilerParams(vmem_limit_bytes=40 * 2**20),
        cost_estimate=pl.CostEstimate(flops=10**10, bytes_accessed=20 * 2**20, transcendentals=0),
        name="score",
    )(slots, recv, stored.reshape(-1, PTOK, DIM))


def local(queries, cand_dev, cand_slot, codes, cent_ids, lengths, centroids, buckets):
    devices = lax.axis_size(AXES)
    q_rows, k_top = cand_dev.shape
    per = cand_slot.shape[1] // k_top
    rows_per = 80
    hits = (cand_dev[:, :, None] == jnp.arange(devices, dtype=jnp.int32)).astype(jnp.int32)
    per_query = jnp.sum(hits, axis=1)
    before = jnp.cumsum(per_query, axis=0) - per_query
    place = jnp.sum(hits * before[:, None, :], axis=2)
    dest = (cand_dev * 2 + place).reshape(-1)
    route = jnp.arange(devices * 2, dtype=jnp.int32)[:, None] == dest[None, :]
    route_q = route.astype(jnp.bfloat16)
    spread = jnp.broadcast_to(
        queries[:, None], (q_rows, k_top) + queries.shape[1:]
    ).reshape(q_rows * k_top, -1)
    send_q = jnp.dot(route_q, spread, preferred_element_type=jnp.float32).astype(jnp.bfloat16)
    slot_rows = cand_slot.reshape(q_rows * k_top, per)
    halves = jnp.concatenate(
        [jnp.bitwise_and(slot_rows, 255), jnp.right_shift(slot_rows, 8)], axis=1
    ).astype(jnp.bfloat16)
    send_s = jnp.dot(route_q, halves, preferred_element_type=jnp.float32).astype(jnp.bfloat16)
    send = jnp.concatenate(
        [
            send_q.reshape(devices, 64, DIM),
            jnp.pad(send_s.reshape(devices, 1, 4 * per), ((0, 0), (0, rows_per - 65), (0, DIM - 4 * per))),
        ],
        axis=1,
    )
    recv = lax.all_to_all(send, AXES, split_axis=0, concat_axis=0, tiled=True)
    stored = unpack(cent_ids, lengths, buckets, codes, centroids)
    got = recv[:, 64, : 4 * per].astype(jnp.int32).reshape(devices * 2, 2 * per)
    slots = (got[:, :per] + 256 * got[:, per:]).reshape(-1)
    scored = score(rows_per, slots, recv.reshape(devices * rows_per, DIM), stored)
    returned = lax.all_to_all(
        scored.reshape(devices, 2, per), AXES, split_axis=0, concat_axis=0, tiled=True
    )
    result = jnp.dot(
        route.astype(jnp.float32).T,
        returned.reshape(devices * 2, per),
        precision=lax.Precision.HIGHEST,
        preferred_element_type=jnp.float32,
    )
    return result.reshape(q_rows, k_top * per)


def solution(mesh):
    in_specs = (
        P(AXES, None, None),
        P(AXES, None),
        P(AXES, None),
        P(AXES, None),
        P(AXES, None),
        P(AXES),
        P(),
        P(),
    )
    return jax.shard_map(
        local, mesh=mesh, in_specs=in_specs, out_specs=P(AXES, None), check_vma=False
    )
```

```python
import functools

import jax
import jax.numpy as jnp
from jax import lax
from jax.experimental import pallas as pl
from jax.experimental.pallas import tpu as pltpu
from jax.sharding import PartitionSpec as P

DIM = 128
PTOK = 128
CHUNK = 32
AXES = ("corpus", "replica")

TAB_STEP = 1024
TAB_BUFS = 10
GROUP_BITS = 3
TURN_BITS = 1
TURN = 1 << TURN_BITS
SCORE_TURN = 8
GROUP = 1 << GROUP_BITS
PARTS = 8


def load_table(cent, tab, buf, sem):
    steps = cent.shape[0] // TAB_STEP

    def copy(i, slot):
        start = pl.multiple_of(i * TAB_STEP, TAB_STEP)
        return pltpu.make_async_copy(cent.at[pl.ds(start, TAB_STEP)], buf.at[slot], sem.at[slot])

    for i in range(min(TAB_BUFS - 1, steps)):
        copy(i, i).start()

    def body(i, carry):
        @pl.when(i + TAB_BUFS - 1 < steps)
        def _():
            copy(i + TAB_BUFS - 1, lax.rem(i + TAB_BUFS - 1, TAB_BUFS)).start()

        slot = lax.rem(i, TAB_BUFS)
        copy(i, slot).wait()
        start = pl.multiple_of(i * TAB_STEP, TAB_STEP)
        tab[pl.ds(start, TAB_STEP), :] = buf[slot].astype(jnp.float32)
        return carry

    lax.fori_loop(0, steps, body, 0)


def unpack_kernel(
    items, starts, lefts, lasts, bounds, buckets, ids_hbm, codes_hbm, cent, out,
    tab, buf, ids, codes, stored, centre, words, raws, squares, spread_of, ones,
    sem, ids_sem, codes_sem, out_sem,
):
    n_items = items.shape[0]
    parts = codes_sem.shape[0]
    code_rows = codes.shape[0] // parts
    part_chunks = n_items // parts

    def codes_copy(j):
        at = pl.ds(pl.multiple_of(j * code_rows, code_rows), code_rows)
        return pltpu.make_async_copy(codes_hbm.at[at], codes.at[at], codes_sem.at[j])

    def out_copy(j):
        at = pl.ds(j * part_chunks, part_chunks)
        return pltpu.make_async_copy(stored.at[at], out.at[at], out_sem)

    ids_copy = pltpu.make_async_copy(ids_hbm, ids, ids_sem)
    ids_copy.start()
    codes_copy(0).start()
    lane = lax.broadcasted_iota(jnp.int32, (8, DIM), 1)
    sub = lax.broadcasted_iota(jnp.int32, (8, DIM), 0)
    low_bit = jnp.left_shift(1, 2 * jnp.bitwise_and(lane, 3))
    high_bit = jnp.left_shift(2, 2 * jnp.bitwise_and(lane, 3))
    source = lax.broadcasted_iota(jnp.int32, (DIM, 4 * DIM), 0)
    target = jnp.right_shift(lax.broadcasted_iota(jnp.int32, (DIM, 4 * DIM), 1), 2)
    spread_of[...] = jnp.where(source == target, 1.0, 0.0).astype(jnp.bfloat16)
    ones[...] = jnp.ones_like(ones)
    centre[1] = jnp.zeros_like(centre[1])
    words[1] = jnp.zeros_like(words[1])
    raws[...] = jnp.zeros_like(raws)
    squares[...] = jnp.zeros_like(squares)
    load_table(cent, tab, buf, sem)
    for j in range(1, parts):
        codes_copy(j).start()
    ids_copy.wait()
    b0, b1, b2, b3 = (buckets[i] for i in range(4))

    def gather(group, side):
        code_rows = []
        for n in range(GROUP):
            item = group * GROUP + n
            code = items[item]
            code_rows.append(codes[pl.ds(starts[item], 8, stride=8), :])
            for k in range(4):
                for r in range(8):
                    token = ids.at[pl.ds((4 * r + k) * n_items, n_items)][code]
                    centre[side, pl.ds(CHUNK * n + 8 * k + r, 1), :] = tab[pl.ds(token, 1), :]
        packed = jnp.concatenate(code_rows, axis=0).astype(jnp.float32).astype(jnp.bfloat16)
        words[side] = jnp.dot(packed, spread_of[...], preferred_element_type=jnp.float32)

    def decode(side):
        for n in range(GROUP):
            parts = []
            for k in range(4):
                at = pl.ds(CHUNK * n + 8 * k, 8)
                word = words[side, pl.ds(8 * n, 8), pl.ds(DIM * k, DIM)].astype(jnp.int32)
                low = jnp.bitwise_and(word, low_bit) != 0
                high = jnp.bitwise_and(word, high_bit) != 0
                residual = jnp.where(high, jnp.where(low, b3, b2), jnp.where(low, b1, b0))
                raw = centre[side, at, :] + residual
                raws[side, at, :] = raw
                parts.append(raw * raw)
            for h in range(2):
                square = jnp.concatenate(parts[2 * h : 2 * h + 2], axis=0)
                top = square.astype(jnp.bfloat16)
                rest = (square - top.astype(jnp.float32)).astype(jnp.bfloat16)
                squares[side, pl.ds(CHUNK * n + 16 * h, 16), :] = jnp.concatenate([top, rest], axis=1)

    def finish(group, side):
        sums = jnp.dot(squares[side], ones[...], preferred_element_type=jnp.float32)
        for n in range(GROUP):
            item = group * GROUP + n
            left = lefts[item]
            embeds = []
            for k in range(4):
                at = CHUNK * n + 8 * k
                total = sums[at : at + 8, :]
                embeds.append(raws[side, pl.ds(at, 8), :] * lax.rsqrt(total + 1e-06))
            first = jnp.broadcast_to(embeds[0][0:1, :], (8, DIM))
            embeds = [jnp.where(4 * sub + k < left, embeds[k], first) for k in range(4)]
            stored[items[item]] = jnp.concatenate(embeds, axis=0).astype(jnp.bfloat16)

    def body(i, carry):
        for turn in range(TURN):
            group = TURN * i + turn
            side = turn % 2
            finish(jnp.clip(group - 2, 0, n_items // GROUP - 1), side)
            decode(1 - side)
            gather(jnp.minimum(group, n_items // GROUP - 1), side)
        return carry

    def repeat(p, carry):
        for q in range(4):
            begin = 4 * (4 * p + q)
            last = lasts[4 * p + q]
            for c in range(1, 4):
                stored[begin + c] = stored[jnp.minimum(begin + c, last)]
        return carry

    n_pass = lasts.shape[0]

    def close(j):
        per = n_pass // parts
        lax.fori_loop(j * (per // 4), (j + 1) * (per // 4), repeat, 0)
        out_copy(j).start()

    def part(j, begin):
        codes_copy(j).wait()
        lax.fori_loop(begin, bounds[j], body, 0)

        @pl.when(j > 0)
        def _():
            close(j - 1)

        return bounds[j]

    lax.fori_loop(0, parts, part, jnp.int32(0))
    close(parts - 1)
    for j in range(parts):
        out_copy(j).wait()


def plan_items(lengths, parts):
    n_pass = lengths.shape[0]
    chunks = jnp.right_shift(lengths + (CHUNK - 1), 5)
    ends = jnp.cumsum(chunks)
    order = jnp.minimum(jnp.arange(4 * n_pass, dtype=jnp.int32), ends[-1] - 1)
    passed = ends[None, :] <= order[:, None]
    which = jnp.sum(passed.astype(jnp.int32), axis=1)
    begin = jnp.max(jnp.where(passed, ends[None, :], 0), axis=1)
    length = jnp.sum(jnp.where(jnp.arange(n_pass)[None, :] == which[:, None], lengths[None, :], 0), axis=1)
    ch = order - begin
    items = 4 * which + ch
    starts = (jnp.right_shift(which, 3) * CHUNK + ch * 8) * 8 + jnp.bitwise_and(which, 7)
    lefts = length - CHUNK * ch
    lasts = 4 * jnp.arange(n_pass, dtype=jnp.int32) + chunks - 1
    per = n_pass // parts
    bounds = jnp.right_shift(ends[per - 1 :: per], GROUP_BITS + TURN_BITS)
    groups = jnp.right_shift(ends[-1] + (GROUP - 1), GROUP_BITS)
    bounds = jnp.where(jnp.arange(parts) == parts - 1, jnp.right_shift(groups + TURN + 1, TURN_BITS), bounds)
    return items, starts, lefts, lasts, bounds


def unpack(ids, lengths, buckets, codes, centroids):
    n_pass = codes.shape[0]
    n_items = 4 * n_pass
    plan = plan_items(lengths, PARTS)
    tiles = codes.reshape(n_pass // 8, 8, CHUNK, DIM).transpose(0, 2, 1, 3).reshape(-1, DIM)
    by_place = ids.reshape(n_items, CHUNK).T.reshape(-1)
    smem = pl.BlockSpec(memory_space=pltpu.SMEM)
    anywhere = pl.BlockSpec(memory_space=pl.ANY)
    rows = GROUP * CHUNK
    return pl.pallas_call(
        unpack_kernel,
        in_specs=[smem] * 6 + [anywhere] * 3,
        out_specs=anywhere,
        out_shape=jax.ShapeDtypeStruct((n_items, CHUNK, DIM), jnp.bfloat16),
        scratch_shapes=[
            pltpu.VMEM(centroids.shape, jnp.float32),
            pltpu.VMEM((TAB_BUFS, TAB_STEP, DIM), jnp.bfloat16),
            pltpu.SMEM((n_pass * PTOK,), jnp.int32),
            pltpu.VMEM(tiles.shape, jnp.int32),
            pltpu.VMEM((n_items, CHUNK, DIM), jnp.bfloat16),
            pltpu.VMEM((2, rows, DIM), jnp.float32),
            pltpu.VMEM((2, 8 * GROUP, 4 * DIM), jnp.float32),
            pltpu.VMEM((2, rows, DIM), jnp.float32),
            pltpu.VMEM((2, rows, 2 * DIM), jnp.bfloat16),
            pltpu.VMEM((DIM, 4 * DIM), jnp.bfloat16),
            pltpu.VMEM((2 * DIM, DIM), jnp.bfloat16),
            pltpu.SemaphoreType.DMA((TAB_BUFS,)),
            pltpu.SemaphoreType.DMA,
            pltpu.SemaphoreType.DMA((PARTS,)),
            pltpu.SemaphoreType.DMA,
        ],
        compiler_params=pltpu.CompilerParams(vmem_limit_bytes=60 * 2**20),
        cost_estimate=pl.CostEstimate(flops=10**9, bytes_accessed=40 * 2**20, transcendentals=0),
        name="unpack",
    )(*plan, buckets, by_place, tiles, centroids)


def score_kernel(rows_per, slots, recv, stored_hbm, out, stored, best, sem):
    parts = sem.shape[0]
    size = stored.shape[0] // parts

    def copy(i):
        return pltpu.make_async_copy(
            stored_hbm.at[pl.ds(i * size, size)], stored.at[pl.ds(i * size, size)], sem.at[i]
        )

    for i in range(parts):
        copy(i).start()
    for i in range(parts):
        copy(i).wait()

    def one(src, which):
        q = recv[pl.ds(pl.multiple_of(src * rows_per + 32 * which, 16), 32), :]
        zero = jnp.zeros_like(q)
        pair_q = jnp.concatenate(
            [jnp.concatenate([q, zero], axis=1), jnp.concatenate([zero, q], axis=1)], axis=0
        )
        query = 2 * src + which
        sides = [[], []]
        for place in range(16):
            sides[place % 2].append(stored[slots[query * 16 + place]])
        both = jnp.concatenate([jnp.concatenate(side, axis=0) for side in sides], axis=1)
        sims = lax.dot_general(
            both, pair_q, (((1,), (1,)), ((), ())), preferred_element_type=jnp.float32
        )
        tops = [
            jnp.max(sims[PTOK * pair : PTOK * (pair + 1), :], axis=0, keepdims=True)
            for pair in range(8)
        ]
        best[pl.ds(query, 1), :] = jnp.concatenate(tops, axis=1)

    def body(src, carry):
        for j in range(SCORE_TURN):
            one(SCORE_TURN * src + j, 0)
            one(SCORE_TURN * src + j, 1)
        return carry

    lax.fori_loop(0, recv.shape[0] // rows_per // SCORE_TURN, body, 0)
    width = best.shape[1]
    member = lax.broadcasted_iota(jnp.int32, (width, 16), 0) // 32
    member = member == lax.broadcasted_iota(jnp.int32, (width, 16), 1)
    out[...] = jnp.dot(
        best[...],
        member.astype(jnp.float32),
        precision=lax.Precision.HIGHEST,
        preferred_element_type=jnp.float32,
    )


def score(rows_per, slots, recv, stored):
    devices = recv.shape[0] // rows_per
    return pl.pallas_call(
        functools.partial(score_kernel, rows_per),
        in_specs=[
            pl.BlockSpec(memory_space=pltpu.SMEM),
            pl.BlockSpec(memory_space=pltpu.VMEM),
            pl.BlockSpec(memory_space=pl.ANY),
        ],
        out_specs=pl.BlockSpec(memory_space=pltpu.VMEM),
        out_shape=jax.ShapeDtypeStruct((2 * devices, 16), jnp.float32),
        scratch_shapes=[
            pltpu.VMEM((stored.size // (PTOK * DIM), PTOK, DIM), jnp.bfloat16),
            pltpu.VMEM((2 * devices, 16 * 32), jnp.float32),
            pltpu.SemaphoreType.DMA((16,)),
        ],
        compiler_params=pltpu.CompilerParams(vmem_limit_bytes=40 * 2**20),
        cost_estimate=pl.CostEstimate(flops=10**10, bytes_accessed=20 * 2**20, transcendentals=0),
        name="score",
    )(slots, recv, stored.reshape(-1, PTOK, DIM))


def local(queries, cand_dev, cand_slot, codes, cent_ids, lengths, centroids, buckets):
    devices = lax.axis_size(AXES)
    q_rows, k_top = cand_dev.shape
    per = cand_slot.shape[1] // k_top
    rows_per = 80
    hits = (cand_dev[:, :, None] == jnp.arange(devices, dtype=jnp.int32)).astype(jnp.int32)
    per_query = jnp.sum(hits, axis=1)
    before = jnp.cumsum(per_query, axis=0) - per_query
    place = jnp.sum(hits * before[:, None, :], axis=2)
    dest = (cand_dev * 2 + place).reshape(-1)
    route = jnp.arange(devices * 2, dtype=jnp.int32)[:, None] == dest[None, :]
    route_q = route.astype(jnp.bfloat16)
    spread = jnp.broadcast_to(
        queries[:, None], (q_rows, k_top) + queries.shape[1:]
    ).reshape(q_rows * k_top, -1)
    send_q = jnp.dot(route_q, spread, preferred_element_type=jnp.float32).astype(jnp.bfloat16)
    slot_rows = cand_slot.reshape(q_rows * k_top, per)
    halves = jnp.concatenate(
        [jnp.bitwise_and(slot_rows, 255), jnp.right_shift(slot_rows, 8)], axis=1
    ).astype(jnp.bfloat16)
    send_s = jnp.dot(route_q, halves, preferred_element_type=jnp.float32).astype(jnp.bfloat16)
    send = jnp.concatenate(
        [
            send_q.reshape(devices, 64, DIM),
            jnp.pad(send_s.reshape(devices, 1, 4 * per), ((0, 0), (0, rows_per - 65), (0, DIM - 4 * per))),
        ],
        axis=1,
    )
    recv = lax.all_to_all(send, AXES, split_axis=0, concat_axis=0, tiled=True)
    stored = unpack(cent_ids, lengths, buckets, codes, centroids)
    got = recv[:, 64, : 4 * per].astype(jnp.int32).reshape(devices * 2, 2 * per)
    slots = (got[:, :per] + 256 * got[:, per:]).reshape(-1)
    scored = score(rows_per, slots, recv.reshape(devices * rows_per, DIM), stored)
    returned = lax.all_to_all(
        scored.reshape(devices, 2, per), AXES, split_axis=0, concat_axis=0, tiled=True
    )
    result = jnp.dot(
        route.astype(jnp.float32).T,
        returned.reshape(devices * 2, per),
        precision=lax.Precision.HIGHEST,
        preferred_element_type=jnp.float32,
    )
    return result.reshape(q_rows, k_top * per)


def solution(mesh):
    in_specs = (
        P(AXES, None, None),
        P(AXES, None),
        P(AXES, None),
        P(AXES, None),
        P(AXES, None),
        P(AXES),
        P(),
        P(),
    )
    return jax.shard_map(
        local, mesh=mesh, in_specs=in_specs, out_specs=P(AXES, None), check_vma=False
    )
```

```python
import functools

import jax
import jax.numpy as jnp
from jax import lax
from jax.experimental import pallas as pl
from jax.experimental.pallas import tpu as pltpu
from jax.sharding import PartitionSpec as P

DIM = 128
PTOK = 128
CHUNK = 32
AXES = ("corpus", "replica")

TAB_STEP = 1024
TAB_BUFS = 10
GROUP_BITS = 3
TURN_BITS = 1
TURN = 1 << TURN_BITS
SCORE_TURN = 8
GROUP = 1 << GROUP_BITS
PARTS = 8
SPARE = 48
SEND_ROWS = 96


def load_table(cent, tab, buf, sem, beside):
    steps = cent.shape[0] // TAB_STEP

    def copy(i, slot):
        start = pl.multiple_of(i * TAB_STEP, TAB_STEP)
        return pltpu.make_async_copy(cent.at[pl.ds(start, TAB_STEP)], buf.at[slot], sem.at[slot])

    for i in range(min(TAB_BUFS - 1, steps)):
        copy(i, i).start()

    def body(i, carry):
        @pl.when(i + TAB_BUFS - 1 < steps)
        def _():
            copy(i + TAB_BUFS - 1, lax.rem(i + TAB_BUFS - 1, TAB_BUFS)).start()

        slot = lax.rem(i, TAB_BUFS)
        copy(i, slot).wait()
        start = pl.multiple_of(i * TAB_STEP, TAB_STEP)
        tab[pl.ds(start, TAB_STEP), :] = buf[slot].astype(jnp.float32)
        return beside(i, carry)

    return lax.fori_loop(0, steps, body, jnp.int32(0))


def unpack_kernel(
    lens, buckets, ids_hbm, codes_hbm, cent, out,
    items, keys, starts, lefts, bounds,
    tab, buf, ids, codes, stored, centre, words, raws, squares, spread_of, ones,
    sem, ids_sem, codes_sem, out_sem,
):
    n_pass = lens.shape[0]
    n_items = 4 * n_pass
    parts = codes_sem.shape[0]
    code_rows = codes.shape[0] // parts
    part_chunks = n_items // parts

    def codes_copy(j):
        at = pl.ds(pl.multiple_of(j * code_rows, code_rows), code_rows)
        return pltpu.make_async_copy(codes_hbm.at[at], codes.at[at], codes_sem.at[j])

    def out_copy(j):
        at = pl.ds(j * part_chunks, part_chunks)
        return pltpu.make_async_copy(stored.at[at], out.at[at], out_sem)

    ids_copy = pltpu.make_async_copy(ids_hbm, ids, ids_sem)
    ids_copy.start()
    codes_copy(0).start()
    lane = lax.broadcasted_iota(jnp.int32, (8, DIM), 1)
    sub = lax.broadcasted_iota(jnp.int32, (8, DIM), 0)
    low_bit = jnp.left_shift(1, 2 * jnp.bitwise_and(lane, 3))
    high_bit = jnp.left_shift(2, 2 * jnp.bitwise_and(lane, 3))
    source = lax.broadcasted_iota(jnp.int32, (DIM, 4 * DIM), 0)
    target = jnp.right_shift(lax.broadcasted_iota(jnp.int32, (DIM, 4 * DIM), 1), 2)
    spread_of[...] = jnp.where(source == target, 1.0, 0.0).astype(jnp.bfloat16)
    ones[...] = jnp.ones_like(ones)
    centre[1] = jnp.zeros_like(centre[1])
    words[1] = jnp.zeros_like(words[1])
    raws[...] = jnp.zeros_like(raws)
    squares[...] = jnp.zeros_like(squares)
    table_steps = cent.shape[0] // TAB_STEP
    per_step = n_pass // table_steps

    def plan(i, count):
        for q in range(per_step):
            p = i * per_step + q
            length = lens[p]
            first = jnp.left_shift(jnp.right_shift(p, 3), 8) + jnp.bitwise_and(p, 7)
            for c in range(4):
                items[count + c] = 4 * p + c
                keys[count + c] = p + c * CHUNK * n_pass
                starts[count + c] = first + 64 * c
                lefts[count + c] = length - CHUNK * c
            count = count + jnp.right_shift(length + (CHUNK - 1), 5)
        bounds[i // (table_steps // parts)] = jnp.right_shift(count, GROUP_BITS + TURN_BITS)
        return count

    count = load_table(cent, tab, buf, sem, plan)
    for extra in range(SPARE):
        for ref in (items, keys, starts, lefts):
            ref[count + extra] = ref[count - 1]
    groups = jnp.right_shift(count + (GROUP - 1), GROUP_BITS)
    bounds[parts - 1] = jnp.right_shift(groups + TURN + 1, TURN_BITS)
    for j in range(1, parts):
        codes_copy(j).start()
    ids_copy.wait()
    b0, b1, b2, b3 = (buckets[i] for i in range(4))

    reach = n_pass * (PTOK - CHUNK + 1)

    def gather(group, side):
        code_rows = []
        for n in range(GROUP):
            item = group * GROUP + n
            key = keys[item]
            code_rows.append(codes[pl.ds(starts[item], 8, stride=8), :])
            for k in range(4):
                for r in range(8):
                    token = ids.at[pl.ds((4 * r + k) * n_pass, reach)][key]
                    centre[side, pl.ds(CHUNK * n + 8 * k + r, 1), :] = tab[pl.ds(token, 1), :]
        packed = jnp.concatenate(code_rows, axis=0).astype(jnp.float32).astype(jnp.bfloat16)
        words[side] = jnp.dot(packed, spread_of[...], preferred_element_type=jnp.float32)

    def decode(side):
        for n in range(GROUP):
            parts = []
            for k in range(4):
                at = pl.ds(CHUNK * n + 8 * k, 8)
                word = words[side, pl.ds(8 * n, 8), pl.ds(DIM * k, DIM)].astype(jnp.int32)
                low = jnp.bitwise_and(word, low_bit) != 0
                high = jnp.bitwise_and(word, high_bit) != 0
                residual = jnp.where(high, jnp.where(low, b3, b2), jnp.where(low, b1, b0))
                raw = centre[side, at, :] + residual
                raws[side, at, :] = raw
                parts.append(raw * raw)
            for h in range(2):
                square = jnp.concatenate(parts[2 * h : 2 * h + 2], axis=0)
                top = square.astype(jnp.bfloat16)
                rest = (square - top.astype(jnp.float32)).astype(jnp.bfloat16)
                squares[side, pl.ds(CHUNK * n + 16 * h, 16), :] = jnp.concatenate([top, rest], axis=1)

    def finish(group, side):
        sums = jnp.dot(squares[side], ones[...], preferred_element_type=jnp.float32)
        for n in range(GROUP):
            item = group * GROUP + n
            left = lefts[item]
            embeds = []
            for k in range(4):
                at = CHUNK * n + 8 * k
                total = sums[at : at + 8, :]
                embeds.append(raws[side, pl.ds(at, 8), :] * lax.rsqrt(total + 1e-06))
            first = jnp.broadcast_to(embeds[0][0:1, :], (8, DIM))
            embeds = [jnp.where(4 * sub + k < left, embeds[k], first) for k in range(4)]
            stored[items[item]] = jnp.concatenate(embeds, axis=0).astype(jnp.bfloat16)

    def body(i, carry):
        for turn in range(TURN):
            group = TURN * i + turn
            side = turn % 2
            finish(jnp.clip(group - 2, 0, n_items // GROUP - 1), side)
            decode(1 - side)
            gather(jnp.minimum(group, n_items // GROUP - 1), side)
        return carry

    def repeat(p, carry):
        for q in range(4):
            begin = 4 * (4 * p + q)
            last = begin + jnp.right_shift(lens[4 * p + q] + (CHUNK - 1), 5) - 1
            for c in range(1, 4):
                stored[begin + c] = stored[jnp.minimum(begin + c, last)]
        return carry

    def close(j):
        per = n_pass // parts
        lax.fori_loop(j * (per // 4), (j + 1) * (per // 4), repeat, 0)
        out_copy(j).start()

    def part(j, begin):
        codes_copy(j).wait()
        lax.fori_loop(begin, bounds[j], body, 0)

        @pl.when(j > 0)
        def _():
            close(j - 1)

        return bounds[j]

    lax.fori_loop(0, parts, part, jnp.int32(0))
    close(parts - 1)
    for j in range(parts):
        out_copy(j).wait()


def unpack(ids, lengths, buckets, codes, centroids):
    n_pass = codes.shape[0]
    n_items = 4 * n_pass
    tiles = codes.reshape(n_pass // 8, 8, CHUNK, DIM).transpose(0, 2, 1, 3).reshape(-1, DIM)
    by_place = ids.T.reshape(-1)
    smem = pl.BlockSpec(memory_space=pltpu.SMEM)
    anywhere = pl.BlockSpec(memory_space=pl.ANY)
    rows = GROUP * CHUNK
    return pl.pallas_call(
        unpack_kernel,
        in_specs=[smem] * 2 + [anywhere] * 3,
        out_specs=anywhere,
        out_shape=jax.ShapeDtypeStruct((n_items, CHUNK, DIM), jnp.bfloat16),
        scratch_shapes=[pltpu.SMEM((n_items + SPARE,), jnp.int32)] * 4
        + [
            pltpu.SMEM((PARTS,), jnp.int32),
            pltpu.VMEM(centroids.shape, jnp.float32),
            pltpu.VMEM((TAB_BUFS, TAB_STEP, DIM), jnp.bfloat16),
            pltpu.SMEM((n_pass * PTOK,), jnp.int32),
            pltpu.VMEM(tiles.shape, jnp.int32),
            pltpu.VMEM((n_items, CHUNK, DIM), jnp.bfloat16),
            pltpu.VMEM((2, rows, DIM), jnp.float32),
            pltpu.VMEM((2, 8 * GROUP, 4 * DIM), jnp.float32),
            pltpu.VMEM((2, rows, DIM), jnp.float32),
            pltpu.VMEM((2, rows, 2 * DIM), jnp.bfloat16),
            pltpu.VMEM((DIM, 4 * DIM), jnp.bfloat16),
            pltpu.VMEM((2 * DIM, DIM), jnp.bfloat16),
            pltpu.SemaphoreType.DMA((TAB_BUFS,)),
            pltpu.SemaphoreType.DMA,
            pltpu.SemaphoreType.DMA((PARTS,)),
            pltpu.SemaphoreType.DMA,
        ],
        compiler_params=pltpu.CompilerParams(vmem_limit_bytes=60 * 2**20),
        cost_estimate=pl.CostEstimate(flops=10**9, bytes_accessed=40 * 2**20, transcendentals=0),
        name="unpack",
    )(lengths, buckets, by_place, tiles, centroids)


def score_kernel(rows_per, slots, recv, stored_hbm, out, stored, best, sem):
    parts = sem.shape[0]
    size = stored.shape[0] // parts

    def copy(i):
        return pltpu.make_async_copy(
            stored_hbm.at[pl.ds(i * size, size)], stored.at[pl.ds(i * size, size)], sem.at[i]
        )

    for i in range(parts):
        copy(i).start()
    for i in range(parts):
        copy(i).wait()

    def one(src, which):
        q = recv[pl.ds(pl.multiple_of(src * rows_per + 32 * which, 16), 32), :]
        zero = jnp.zeros_like(q)
        pair_q = jnp.concatenate(
            [jnp.concatenate([q, zero], axis=1), jnp.concatenate([zero, q], axis=1)], axis=0
        )
        query = 2 * src + which
        sides = [[], []]
        for place in range(16):
            sides[place % 2].append(stored[slots[query * 16 + place]])
        both = jnp.concatenate([jnp.concatenate(side, axis=0) for side in sides], axis=1)
        sims = lax.dot_general(
            both, pair_q, (((1,), (1,)), ((), ())), preferred_element_type=jnp.float32
        )
        tops = [
            jnp.max(sims[PTOK * pair : PTOK * (pair + 1), :], axis=0, keepdims=True)
            for pair in range(8)
        ]
        best[pl.ds(query, 1), :] = jnp.concatenate(tops, axis=1)

    def body(src, carry):
        for j in range(SCORE_TURN):
            one(SCORE_TURN * src + j, 0)
            one(SCORE_TURN * src + j, 1)
        return carry

    lax.fori_loop(0, recv.shape[0] // rows_per // SCORE_TURN, body, 0)
    width = best.shape[1]
    member = lax.broadcasted_iota(jnp.int32, (width, 16), 0) // 32
    member = member == lax.broadcasted_iota(jnp.int32, (width, 16), 1)
    out[...] = jnp.dot(
        best[...],
        member.astype(jnp.float32),
        precision=lax.Precision.HIGHEST,
        preferred_element_type=jnp.float32,
    )


def score(rows_per, slots, recv, stored):
    devices = recv.shape[0] // rows_per
    return pl.pallas_call(
        functools.partial(score_kernel, rows_per),
        in_specs=[
            pl.BlockSpec(memory_space=pltpu.SMEM),
            pl.BlockSpec(memory_space=pltpu.VMEM),
            pl.BlockSpec(memory_space=pl.ANY),
        ],
        out_specs=pl.BlockSpec(memory_space=pltpu.VMEM),
        out_shape=jax.ShapeDtypeStruct((2 * devices, 16), jnp.float32),
        scratch_shapes=[
            pltpu.VMEM((stored.size // (PTOK * DIM), PTOK, DIM), jnp.bfloat16),
            pltpu.VMEM((2 * devices, 16 * 32), jnp.float32),
            pltpu.SemaphoreType.DMA((16,)),
        ],
        compiler_params=pltpu.CompilerParams(vmem_limit_bytes=40 * 2**20),
        cost_estimate=pl.CostEstimate(flops=10**10, bytes_accessed=20 * 2**20, transcendentals=0),
        name="score",
    )(slots, recv, stored.reshape(-1, PTOK, DIM))


def address_kernel(cand, queries, slots, send, dest, seen):
    devices = seen.shape[0]
    q_rows, k_top = cand.shape
    per = slots.shape[1] // k_top
    send[...] = jnp.zeros_like(send)
    for d in range(devices):
        seen[d] = 0
    listed = slots[...]
    low = jnp.bitwise_and(listed, 255).astype(jnp.float32)
    high = jnp.right_shift(listed, 8).astype(jnp.float32)
    in_row = DIM // per
    for t in range(k_top):
        row = t // in_row
        turn = (in_row - t % in_row) * per % DIM
        pieces = [
            pltpu.roll(part[:, row * DIM : (row + 1) * DIM], turn, 1) if turn else part[:, row * DIM : (row + 1) * DIM]
            for part in (low, high)
        ]
        for q in range(q_rows):
            device = cand[q, t]
            place = seen[device]
            seen[device] = 1
            dest[q * k_top + t] = 2 * device + place
            base = pl.multiple_of(device * SEND_ROWS + 32 * place, 16)
            send[pl.ds(base, 32), :] = queries[q]
            meta = [jnp.broadcast_to(piece[q : q + 1, :], (8, DIM)) for piece in pieces]
            at = pl.multiple_of(device * SEND_ROWS + 64 + 16 * place, 16)
            send[pl.ds(at, 16), :] = jnp.concatenate(meta, axis=0).astype(jnp.bfloat16)


def address(cand_dev, queries, cand_slot, devices):
    smem = pl.BlockSpec(memory_space=pltpu.SMEM)
    vmem = pl.BlockSpec(memory_space=pltpu.VMEM)
    return pl.pallas_call(
        address_kernel,
        in_specs=[smem, vmem, vmem],
        out_specs=[vmem, smem],
        out_shape=[
            jax.ShapeDtypeStruct((devices * SEND_ROWS, DIM), jnp.bfloat16),
            jax.ShapeDtypeStruct((cand_dev.size,), jnp.int32),
        ],
        scratch_shapes=[pltpu.SMEM((devices,), jnp.int32)],
        compiler_params=pltpu.CompilerParams(vmem_limit_bytes=24 * 2**20),
        name="address",
    )(cand_dev, queries, cand_slot)


def local(queries, cand_dev, cand_slot, codes, cent_ids, lengths, centroids, buckets):
    devices = lax.axis_size(AXES)
    q_rows, k_top = cand_dev.shape
    per = cand_slot.shape[1] // k_top
    send, dest = address(cand_dev, queries, cand_slot, devices)
    recv = lax.all_to_all(
        send.reshape(devices, SEND_ROWS, DIM), AXES, split_axis=0, concat_axis=0, tiled=True
    )
    stored = unpack(cent_ids, lengths, buckets, codes, centroids)
    got = recv.reshape(devices, SEND_ROWS // 8, 8, DIM)[:, 8:, 0, :per].astype(jnp.int32)
    slots = (got[:, 0::2] + 256 * got[:, 1::2]).reshape(-1)
    scored = score(SEND_ROWS, slots, recv.reshape(devices * SEND_ROWS, DIM), stored)
    returned = lax.all_to_all(
        scored.reshape(devices, 2, per), AXES, split_axis=0, concat_axis=0, tiled=True
    )
    route = jnp.arange(devices * 2, dtype=jnp.int32)[None, :] == dest[:, None]
    result = jnp.dot(
        route.astype(jnp.float32),
        returned.reshape(devices * 2, per),
        precision=lax.Precision.HIGHEST,
        preferred_element_type=jnp.float32,
    )
    return result.reshape(q_rows, k_top * per)


def solution(mesh):
    in_specs = (
        P(AXES, None, None),
        P(AXES, None),
        P(AXES, None),
        P(AXES, None),
        P(AXES, None),
        P(AXES),
        P(),
        P(),
    )
    return jax.shard_map(
        local, mesh=mesh, in_specs=in_specs, out_specs=P(AXES, None), check_vma=False
    )
```

```python
import functools

import jax
import jax.numpy as jnp
from jax import lax
from jax.experimental import pallas as pl
from jax.experimental.pallas import tpu as pltpu
from jax.sharding import PartitionSpec as P

DIM = 128
PTOK = 128
CHUNK = 32
AXES = ("corpus", "replica")

TAB_STEP = 1024
TAB_BUFS = 10
GROUP_BITS = 3
TURN_BITS = 1
TURN = 1 << TURN_BITS
SCORE_TURN = 16
GROUP = 1 << GROUP_BITS
PARTS = 8
SPARE = 48
SEND_ROWS = 96


def load_table(cent, tab, buf, sem, beside):
    steps = cent.shape[0] // TAB_STEP

    def copy(i, slot):
        start = pl.multiple_of(i * TAB_STEP, TAB_STEP)
        return pltpu.make_async_copy(cent.at[pl.ds(start, TAB_STEP)], buf.at[slot], sem.at[slot])

    for i in range(min(TAB_BUFS - 1, steps)):
        copy(i, i).start()

    def body(i, carry):
        @pl.when(i + TAB_BUFS - 1 < steps)
        def _():
            copy(i + TAB_BUFS - 1, lax.rem(i + TAB_BUFS - 1, TAB_BUFS)).start()

        slot = lax.rem(i, TAB_BUFS)
        copy(i, slot).wait()
        start = pl.multiple_of(i * TAB_STEP, TAB_STEP)
        tab[pl.ds(start, TAB_STEP), :] = buf[slot].astype(jnp.float32)
        return beside(i, carry)

    return lax.fori_loop(0, steps, body, jnp.int32(0))


def unpack_kernel(
    lens, buckets, ids_hbm, codes_hbm, cent, out,
    items, keys, starts, lefts, bounds,
    tab, buf, ids, codes, stored, centre, words, raws, squares, spread_of, ones,
    sem, ids_sem, codes_sem, out_sem,
):
    n_pass = lens.shape[0]
    n_items = 4 * n_pass
    parts = codes_sem.shape[0]
    code_rows = codes.shape[0] // parts
    part_chunks = n_items // parts

    def codes_copy(j):
        at = pl.ds(pl.multiple_of(j * code_rows, code_rows), code_rows)
        return pltpu.make_async_copy(codes_hbm.at[at], codes.at[at], codes_sem.at[j])

    def out_copy(j):
        at = pl.ds(j * part_chunks, part_chunks)
        return pltpu.make_async_copy(stored.at[at], out.at[at], out_sem)

    ids_copy = pltpu.make_async_copy(ids_hbm, ids, ids_sem)
    ids_copy.start()
    codes_copy(0).start()
    lane = lax.broadcasted_iota(jnp.int32, (8, DIM), 1)
    sub = lax.broadcasted_iota(jnp.int32, (8, DIM), 0)
    low_bit = jnp.left_shift(1, 2 * jnp.bitwise_and(lane, 3))
    high_bit = jnp.left_shift(2, 2 * jnp.bitwise_and(lane, 3))
    source = lax.broadcasted_iota(jnp.int32, (DIM, 4 * DIM), 0)
    target = jnp.right_shift(lax.broadcasted_iota(jnp.int32, (DIM, 4 * DIM), 1), 2)
    spread_of[...] = jnp.where(source == target, 1.0, 0.0).astype(jnp.bfloat16)
    ones[...] = jnp.ones_like(ones)
    centre[1] = jnp.zeros_like(centre[1])
    words[1] = jnp.zeros_like(words[1])
    raws[...] = jnp.zeros_like(raws)
    squares[...] = jnp.zeros_like(squares)
    table_steps = cent.shape[0] // TAB_STEP
    per_step = n_pass // table_steps

    def plan(i, count):
        for q in range(per_step):
            p = i * per_step + q
            length = lens[p]
            first = jnp.left_shift(jnp.right_shift(p, 3), 8) + jnp.bitwise_and(p, 7)
            for c in range(4):
                for ref, value in (
                    (items, 4 * p + c),
                    (keys, p + c * CHUNK * n_pass),
                    (starts, first + 64 * c),
                    (lefts, length - CHUNK * c),
                ):
                    ref.at[pl.ds(c, n_items)][count] = value
            count = count + jnp.right_shift(length + (CHUNK - 1), 5)
        bounds[i // (table_steps // parts)] = jnp.right_shift(count, GROUP_BITS + TURN_BITS)
        return count

    count = load_table(cent, tab, buf, sem, plan)
    for extra in range(SPARE):
        for ref in (items, keys, starts, lefts):
            ref[count + extra] = ref[count - 1]
    groups = jnp.right_shift(count + (GROUP - 1), GROUP_BITS)
    bounds[parts - 1] = jnp.right_shift(groups + TURN + 1, TURN_BITS)
    for j in range(1, parts):
        codes_copy(j).start()
    ids_copy.wait()
    b0, b1, b2, b3 = (buckets[i] for i in range(4))

    reach = n_pass * (PTOK - CHUNK + 1)

    def gather(group, side):
        code_rows = []
        for n in range(GROUP):
            at = pl.ds(n, n_items)
            key = keys.at[at][group * GROUP]
            code_rows.append(codes[pl.ds(starts.at[at][group * GROUP], 8, stride=8), :])
            for k in range(4):
                for r in range(8):
                    token = ids.at[pl.ds((4 * r + k) * n_pass, reach)][key]
                    centre[side, pl.ds(CHUNK * n + 8 * k + r, 1), :] = tab[pl.ds(token, 1), :]
        packed = jnp.concatenate(code_rows, axis=0).astype(jnp.float32).astype(jnp.bfloat16)
        words[side] = jnp.dot(packed, spread_of[...], preferred_element_type=jnp.float32)

    def decode(side):
        for n in range(GROUP):
            parts = []
            for k in range(4):
                at = pl.ds(CHUNK * n + 8 * k, 8)
                word = words[side, pl.ds(8 * n, 8), pl.ds(DIM * k, DIM)].astype(jnp.int32)
                low = jnp.bitwise_and(word, low_bit) != 0
                high = jnp.bitwise_and(word, high_bit) != 0
                residual = jnp.where(high, jnp.where(low, b3, b2), jnp.where(low, b1, b0))
                raw = centre[side, at, :] + residual
                raws[side, at, :] = raw
                parts.append(raw * raw)
            for h in range(2):
                square = jnp.concatenate(parts[2 * h : 2 * h + 2], axis=0)
                top = square.astype(jnp.bfloat16)
                rest = (square - top.astype(jnp.float32)).astype(jnp.bfloat16)
                squares[side, pl.ds(CHUNK * n + 16 * h, 16), :] = jnp.concatenate([top, rest], axis=1)

    def finish(group, side):
        sums = jnp.dot(squares[side], ones[...], preferred_element_type=jnp.float32)
        for n in range(GROUP):
            entry = pl.ds(n, n_items)
            left = lefts.at[entry][group * GROUP]
            embeds = []
            for k in range(4):
                at = CHUNK * n + 8 * k
                total = sums[at : at + 8, :]
                embeds.append(raws[side, pl.ds(at, 8), :] * lax.rsqrt(total + 1e-06))
            first = jnp.broadcast_to(embeds[0][0:1, :], (8, DIM))
            embeds = [jnp.where(4 * sub + k < left, embeds[k], first) for k in range(4)]
            stored[items.at[entry][group * GROUP]] = jnp.concatenate(embeds, axis=0).astype(jnp.bfloat16)

    def body(i, carry):
        for turn in range(TURN):
            group = TURN * i + turn
            side = turn % 2
            finish(jnp.clip(group - 2, 0, n_items // GROUP - 1), side)
            decode(1 - side)
            gather(jnp.minimum(group, n_items // GROUP - 1), side)
        return carry

    def repeat(p, carry):
        for q in range(4):
            begin = 4 * (4 * p + q)
            last = begin + jnp.right_shift(lens[4 * p + q] + (CHUNK - 1), 5) - 1
            for c in range(1, 4):
                stored[begin + c] = stored[jnp.minimum(begin + c, last)]
        return carry

    def close(j):
        per = n_pass // parts
        lax.fori_loop(j * (per // 4), (j + 1) * (per // 4), repeat, 0)
        out_copy(j).start()

    def part(j, begin):
        codes_copy(j).wait()
        lax.fori_loop(begin, bounds[j], body, 0)

        @pl.when(j > 0)
        def _():
            close(j - 1)

        return bounds[j]

    lax.fori_loop(0, parts, part, jnp.int32(0))
    close(parts - 1)
    for j in range(parts):
        out_copy(j).wait()


def unpack(ids, lengths, buckets, codes, centroids):
    n_pass = codes.shape[0]
    n_items = 4 * n_pass
    tiles = codes.reshape(n_pass // 8, 8, CHUNK, DIM).transpose(0, 2, 1, 3).reshape(-1, DIM)
    by_place = ids.T.reshape(-1)
    smem = pl.BlockSpec(memory_space=pltpu.SMEM)
    anywhere = pl.BlockSpec(memory_space=pl.ANY)
    rows = GROUP * CHUNK
    return pl.pallas_call(
        unpack_kernel,
        in_specs=[smem] * 2 + [anywhere] * 3,
        out_specs=anywhere,
        out_shape=jax.ShapeDtypeStruct((n_items, CHUNK, DIM), jnp.bfloat16),
        scratch_shapes=[pltpu.SMEM((n_items + SPARE,), jnp.int32)] * 4
        + [
            pltpu.SMEM((PARTS,), jnp.int32),
            pltpu.VMEM(centroids.shape, jnp.float32),
            pltpu.VMEM((TAB_BUFS, TAB_STEP, DIM), jnp.bfloat16),
            pltpu.SMEM((n_pass * PTOK,), jnp.int32),
            pltpu.VMEM(tiles.shape, jnp.int32),
            pltpu.VMEM((n_items, CHUNK, DIM), jnp.bfloat16),
            pltpu.VMEM((2, rows, DIM), jnp.float32),
            pltpu.VMEM((2, 8 * GROUP, 4 * DIM), jnp.float32),
            pltpu.VMEM((2, rows, DIM), jnp.float32),
            pltpu.VMEM((2, rows, 2 * DIM), jnp.bfloat16),
            pltpu.VMEM((DIM, 4 * DIM), jnp.bfloat16),
            pltpu.VMEM((2 * DIM, DIM), jnp.bfloat16),
            pltpu.SemaphoreType.DMA((TAB_BUFS,)),
            pltpu.SemaphoreType.DMA,
            pltpu.SemaphoreType.DMA((PARTS,)),
            pltpu.SemaphoreType.DMA,
        ],
        compiler_params=pltpu.CompilerParams(vmem_limit_bytes=60 * 2**20),
        cost_estimate=pl.CostEstimate(flops=10**9, bytes_accessed=40 * 2**20, transcendentals=0),
        name="unpack",
    )(lengths, buckets, by_place, tiles, centroids)


def score_kernel(rows_per, recv, stored_hbm, out, stored, best, listed, slots, sem, slots_sem):
    parts = sem.shape[0]
    size = stored.shape[0] // parts

    def copy(i):
        return pltpu.make_async_copy(
            stored_hbm.at[pl.ds(i * size, size)], stored.at[pl.ds(i * size, size)], sem.at[i]
        )

    for i in range(parts):
        copy(i).start()

    def read(src, carry):
        for which in range(2):
            at = pl.multiple_of(src * rows_per + 64 + 16 * which, 16)
            meta = recv[pl.ds(at, 16), :].astype(jnp.float32)
            slot = meta[0:1, :] + 256.0 * meta[8:9, :]
            listed[pl.ds(2 * src + which, 1), :] = slot.astype(jnp.int32)
        return carry

    lax.fori_loop(0, recv.shape[0] // rows_per, read, 0)
    slots_copy = pltpu.make_async_copy(listed, slots, slots_sem)
    slots_copy.start()
    slots_copy.wait()
    for i in range(parts):
        copy(i).wait()

    def one(src, which):
        q = recv[pl.ds(pl.multiple_of(src * rows_per + 32 * which, 16), 32), :]
        zero = jnp.zeros_like(q)
        pair_q = jnp.concatenate(
            [jnp.concatenate([q, zero], axis=1), jnp.concatenate([zero, q], axis=1)], axis=0
        )
        query = 2 * src + which
        sides = [[], []]
        for place in range(16):
            sides[place % 2].append(stored[slots[query, place]])
        both = jnp.concatenate([jnp.concatenate(side, axis=0) for side in sides], axis=1)
        sims = lax.dot_general(
            both, pair_q, (((1,), (1,)), ((), ())), preferred_element_type=jnp.float32
        )
        tops = [
            jnp.max(sims[PTOK * pair : PTOK * (pair + 1), :], axis=0, keepdims=True)
            for pair in range(8)
        ]
        best[pl.ds(query, 1), :] = jnp.concatenate(tops, axis=1)

    def body(src, carry):
        for j in range(SCORE_TURN):
            one(SCORE_TURN * src + j, 0)
            one(SCORE_TURN * src + j, 1)
        return carry

    lax.fori_loop(0, recv.shape[0] // rows_per // SCORE_TURN, body, 0)
    width = best.shape[1]
    member = lax.broadcasted_iota(jnp.int32, (width, 16), 0) // 32
    member = member == lax.broadcasted_iota(jnp.int32, (width, 16), 1)
    out[...] = jnp.dot(
        best[...],
        member.astype(jnp.float32),
        precision=lax.Precision.HIGHEST,
        preferred_element_type=jnp.float32,
    )


def score(rows_per, recv, stored):
    devices = recv.shape[0] // rows_per
    return pl.pallas_call(
        functools.partial(score_kernel, rows_per),
        in_specs=[
            pl.BlockSpec(memory_space=pltpu.VMEM),
            pl.BlockSpec(memory_space=pl.ANY),
        ],
        out_specs=pl.BlockSpec(memory_space=pltpu.VMEM),
        out_shape=jax.ShapeDtypeStruct((2 * devices, 16), jnp.float32),
        scratch_shapes=[
            pltpu.VMEM((stored.size // (PTOK * DIM), PTOK, DIM), jnp.bfloat16),
            pltpu.VMEM((2 * devices, 16 * 32), jnp.float32),
            pltpu.VMEM((2 * devices, DIM), jnp.int32),
            pltpu.SMEM((2 * devices, DIM), jnp.int32),
            pltpu.SemaphoreType.DMA((16,)),
            pltpu.SemaphoreType.DMA,
        ],
        compiler_params=pltpu.CompilerParams(vmem_limit_bytes=40 * 2**20),
        cost_estimate=pl.CostEstimate(flops=10**10, bytes_accessed=20 * 2**20, transcendentals=0),
        name="score",
    )(recv, stored.reshape(-1, PTOK, DIM))


def address_kernel(cand, queries, slots, send, dest, seen):
    devices = seen.shape[0]
    q_rows, k_top = cand.shape
    per = slots.shape[1] // k_top
    send[...] = jnp.zeros_like(send)
    for d in range(devices):
        seen[d] = 0
    listed = slots[...]
    low = jnp.bitwise_and(listed, 255).astype(jnp.float32)
    high = jnp.right_shift(listed, 8).astype(jnp.float32)
    in_row = DIM // per
    for t in range(k_top):
        row = t // in_row
        turn = (in_row - t % in_row) * per % DIM
        pieces = [
            pltpu.roll(part[:, row * DIM : (row + 1) * DIM], turn, 1) if turn else part[:, row * DIM : (row + 1) * DIM]
            for part in (low, high)
        ]
        for q in range(q_rows):
            device = cand[q, t]
            place = seen[device]
            seen[device] = 1
            dest[q * k_top + t] = 2 * device + place
            base = pl.multiple_of(device * SEND_ROWS + 32 * place, 16)
            send[pl.ds(base, 32), :] = queries[q]
            meta = [jnp.broadcast_to(piece[q : q + 1, :], (8, DIM)) for piece in pieces]
            at = pl.multiple_of(device * SEND_ROWS + 64 + 16 * place, 16)
            send[pl.ds(at, 16), :] = jnp.concatenate(meta, axis=0).astype(jnp.bfloat16)


def address(cand_dev, queries, cand_slot, devices):
    smem = pl.BlockSpec(memory_space=pltpu.SMEM)
    vmem = pl.BlockSpec(memory_space=pltpu.VMEM)
    return pl.pallas_call(
        address_kernel,
        in_specs=[smem, vmem, vmem],
        out_specs=[vmem, smem],
        out_shape=[
            jax.ShapeDtypeStruct((devices * SEND_ROWS, DIM), jnp.bfloat16),
            jax.ShapeDtypeStruct((cand_dev.size,), jnp.int32),
        ],
        scratch_shapes=[pltpu.SMEM((devices,), jnp.int32)],
        compiler_params=pltpu.CompilerParams(vmem_limit_bytes=24 * 2**20),
        name="address",
    )(cand_dev, queries, cand_slot)


def local(queries, cand_dev, cand_slot, codes, cent_ids, lengths, centroids, buckets):
    devices = lax.axis_size(AXES)
    q_rows, k_top = cand_dev.shape
    per = cand_slot.shape[1] // k_top
    send, dest = address(cand_dev, queries, cand_slot, devices)
    recv = lax.all_to_all(
        send.reshape(devices, SEND_ROWS, DIM), AXES, split_axis=0, concat_axis=0, tiled=True
    )
    stored = unpack(cent_ids, lengths, buckets, codes, centroids)
    scored = score(SEND_ROWS, recv.reshape(devices * SEND_ROWS, DIM), stored)
    returned = lax.all_to_all(
        scored.reshape(devices, 2, per), AXES, split_axis=0, concat_axis=0, tiled=True
    )
    route = jnp.arange(devices * 2, dtype=jnp.int32)[None, :] == dest[:, None]
    result = jnp.dot(
        route.astype(jnp.float32),
        returned.reshape(devices * 2, per),
        precision=lax.Precision.HIGHEST,
        preferred_element_type=jnp.float32,
    )
    return result.reshape(q_rows, k_top * per)


def solution(mesh):
    in_specs = (
        P(AXES, None, None),
        P(AXES, None),
        P(AXES, None),
        P(AXES, None),
        P(AXES, None),
        P(AXES),
        P(),
        P(),
    )
    return jax.shard_map(
        local, mesh=mesh, in_specs=in_specs, out_specs=P(AXES, None), check_vma=False
    )
```

```python
import functools

import jax
import jax.numpy as jnp
from jax import lax
from jax.experimental import pallas as pl
from jax.experimental.pallas import tpu as pltpu
from jax.sharding import PartitionSpec as P

DIM = 128
PTOK = 128
CHUNK = 32
AXES = ("corpus", "replica")

TAB_STEP = 1024
TAB_BUFS = 10
GROUP_BITS = 3
TURN_BITS = 1
TURN = 1 << TURN_BITS
SCORE_TURN = 16
GROUP = 1 << GROUP_BITS
PARTS = 16
SPARE = 48
SEND_ROWS = 96


def load_table(cent, tab, buf, sem, beside):
    steps = cent.shape[0] // TAB_STEP

    def copy(i, slot):
        start = pl.multiple_of(i * TAB_STEP, TAB_STEP)
        return pltpu.make_async_copy(cent.at[pl.ds(start, TAB_STEP)], buf.at[slot], sem.at[slot])

    for i in range(min(TAB_BUFS - 1, steps)):
        copy(i, i).start()

    def body(i, carry):
        @pl.when(i + TAB_BUFS - 1 < steps)
        def _():
            copy(i + TAB_BUFS - 1, lax.rem(i + TAB_BUFS - 1, TAB_BUFS)).start()

        slot = lax.rem(i, TAB_BUFS)
        copy(i, slot).wait()
        start = pl.multiple_of(i * TAB_STEP, TAB_STEP)
        tab[pl.ds(start, TAB_STEP), :] = buf[slot].astype(jnp.float32)
        return beside(i, carry)

    return lax.fori_loop(0, steps, body, jnp.int32(0))


def unpack_kernel(
    lens, buckets, ids_hbm, codes_hbm, cent, out,
    items, keys, starts, lefts, bounds,
    tab, buf, ids, codes, stored, centre, words, raws, squares, spread_of, ones,
    sem, ids_sem, codes_sem, out_sem,
):
    n_pass = lens.shape[0]
    n_items = 4 * n_pass
    parts = codes_sem.shape[0]
    code_rows = codes.shape[0] // parts
    part_chunks = n_items // parts

    def codes_copy(j):
        at = pl.ds(pl.multiple_of(j * code_rows, code_rows), code_rows)
        return pltpu.make_async_copy(codes_hbm.at[at], codes.at[at], codes_sem.at[j])

    def out_copy(j):
        at = pl.ds(j * part_chunks, part_chunks)
        return pltpu.make_async_copy(stored.at[at], out.at[at], out_sem)

    ids_copy = pltpu.make_async_copy(ids_hbm, ids, ids_sem)
    ids_copy.start()
    codes_copy(0).start()
    lane = lax.broadcasted_iota(jnp.int32, (8, DIM), 1)
    sub = lax.broadcasted_iota(jnp.int32, (8, DIM), 0)
    low_bit = jnp.left_shift(1, 2 * jnp.bitwise_and(lane, 3))
    high_bit = jnp.left_shift(2, 2 * jnp.bitwise_and(lane, 3))
    source = lax.broadcasted_iota(jnp.int32, (DIM, 4 * DIM), 0)
    target = jnp.right_shift(lax.broadcasted_iota(jnp.int32, (DIM, 4 * DIM), 1), 2)
    spread_of[...] = jnp.where(source == target, 1.0, 0.0).astype(jnp.bfloat16)
    ones[...] = jnp.ones_like(ones)
    centre[1] = jnp.zeros_like(centre[1])
    words[1] = jnp.zeros_like(words[1])
    raws[...] = jnp.zeros_like(raws)
    squares[...] = jnp.zeros_like(squares)
    table_steps = cent.shape[0] // TAB_STEP
    per_step = n_pass // table_steps

    def plan(i, count):
        for q in range(per_step):
            p = i * per_step + q
            length = lens[p]
            first = jnp.left_shift(jnp.right_shift(p, 3), 8) + jnp.bitwise_and(p, 7)
            for c in range(4):
                for ref, value in (
                    (items, 4 * p + c),
                    (keys, p + c * CHUNK * n_pass),
                    (starts, first + 64 * c),
                    (lefts, length - CHUNK * c),
                ):
                    ref.at[pl.ds(c, n_items)][count] = value
            count = count + jnp.right_shift(length + (CHUNK - 1), 5)
        bounds[i // (table_steps // parts)] = jnp.right_shift(count, GROUP_BITS + TURN_BITS)
        return count

    count = load_table(cent, tab, buf, sem, plan)
    for extra in range(SPARE):
        for ref in (items, keys, starts, lefts):
            ref[count + extra] = ref[count - 1]
    groups = jnp.right_shift(count + (GROUP - 1), GROUP_BITS)
    bounds[parts - 1] = jnp.right_shift(groups + TURN + 1, TURN_BITS)
    for j in range(1, parts):
        codes_copy(j).start()
    ids_copy.wait()
    b0, b1, b2, b3 = (buckets[i] for i in range(4))

    reach = n_pass * (PTOK - CHUNK + 1)

    def gather(group, side):
        code_rows = []
        for n in range(GROUP):
            at = pl.ds(n, n_items)
            key = keys.at[at][group * GROUP]
            code_rows.append(codes[pl.ds(starts.at[at][group * GROUP], 8, stride=8), :])
            for k in range(4):
                for r in range(8):
                    token = ids.at[pl.ds((4 * r + k) * n_pass, reach)][key]
                    centre[side, pl.ds(CHUNK * n + 8 * k + r, 1), :] = tab[pl.ds(token, 1), :]
        packed = jnp.concatenate(code_rows, axis=0).astype(jnp.float32).astype(jnp.bfloat16)
        words[side] = jnp.dot(packed, spread_of[...], preferred_element_type=jnp.float32)

    def decode(side):
        for n in range(GROUP):
            parts = []
            for k in range(4):
                at = pl.ds(CHUNK * n + 8 * k, 8)
                word = words[side, pl.ds(8 * n, 8), pl.ds(DIM * k, DIM)].astype(jnp.int32)
                low = jnp.bitwise_and(word, low_bit) != 0
                high = jnp.bitwise_and(word, high_bit) != 0
                residual = jnp.where(high, jnp.where(low, b3, b2), jnp.where(low, b1, b0))
                raw = centre[side, at, :] + residual
                raws[side, at, :] = raw
                parts.append(raw * raw)
            for h in range(2):
                square = jnp.concatenate(parts[2 * h : 2 * h + 2], axis=0)
                top = square.astype(jnp.bfloat16)
                rest = (square - top.astype(jnp.float32)).astype(jnp.bfloat16)
                squares[side, pl.ds(CHUNK * n + 16 * h, 16), :] = jnp.concatenate([top, rest], axis=1)

    def finish(group, side):
        sums = jnp.dot(squares[side], ones[...], preferred_element_type=jnp.float32)
        for n in range(GROUP):
            entry = pl.ds(n, n_items)
            left = lefts.at[entry][group * GROUP]
            embeds = []
            for k in range(4):
                at = CHUNK * n + 8 * k
                total = sums[at : at + 8, :]
                embeds.append(raws[side, pl.ds(at, 8), :] * lax.rsqrt(total + 1e-06))
            first = jnp.broadcast_to(embeds[0][0:1, :], (8, DIM))
            embeds = [jnp.where(4 * sub + k < left, embeds[k], first) for k in range(4)]
            stored[items.at[entry][group * GROUP]] = jnp.concatenate(embeds, axis=0).astype(jnp.bfloat16)

    def body(i, carry):
        for turn in range(TURN):
            group = TURN * i + turn
            side = turn % 2
            finish(jnp.clip(group - 2, 0, n_items // GROUP - 1), side)
            decode(1 - side)
            gather(jnp.minimum(group, n_items // GROUP - 1), side)
        return carry

    def repeat(p, carry):
        block = stored.at[pl.ds(16 * p, 16)]
        for q in range(4):
            last = jnp.right_shift(lens.at[pl.ds(q, n_pass - 3)][4 * p] + (CHUNK - 1), 5) - 1
            for c in range(1, 4):
                block[4 * q + c] = block[4 * q + jnp.minimum(last, c)]
        return carry

    def close(j):
        per = n_pass // parts
        lax.fori_loop(j * (per // 4), (j + 1) * (per // 4), repeat, 0)
        out_copy(j).start()

    def part(j, begin):
        codes_copy(j).wait()
        lax.fori_loop(begin, bounds[j], body, 0)

        @pl.when(j > 0)
        def _():
            close(j - 1)

        return bounds[j]

    lax.fori_loop(0, parts, part, jnp.int32(0))
    close(parts - 1)
    for j in range(parts):
        out_copy(j).wait()


def unpack(ids, lengths, buckets, codes, centroids):
    n_pass = codes.shape[0]
    n_items = 4 * n_pass
    tiles = codes.reshape(n_pass // 8, 8, CHUNK, DIM).transpose(0, 2, 1, 3).reshape(-1, DIM)
    by_place = ids.T.reshape(-1)
    smem = pl.BlockSpec(memory_space=pltpu.SMEM)
    anywhere = pl.BlockSpec(memory_space=pl.ANY)
    rows = GROUP * CHUNK
    return pl.pallas_call(
        unpack_kernel,
        in_specs=[smem] * 2 + [anywhere] * 3,
        out_specs=anywhere,
        out_shape=jax.ShapeDtypeStruct((n_items, CHUNK, DIM), jnp.bfloat16),
        scratch_shapes=[pltpu.SMEM((n_items + SPARE,), jnp.int32)] * 4
        + [
            pltpu.SMEM((PARTS,), jnp.int32),
            pltpu.VMEM(centroids.shape, jnp.float32),
            pltpu.VMEM((TAB_BUFS, TAB_STEP, DIM), jnp.bfloat16),
            pltpu.SMEM((n_pass * PTOK,), jnp.int32),
            pltpu.VMEM(tiles.shape, jnp.int32),
            pltpu.VMEM((n_items, CHUNK, DIM), jnp.bfloat16),
            pltpu.VMEM((2, rows, DIM), jnp.float32),
            pltpu.VMEM((2, 8 * GROUP, 4 * DIM), jnp.float32),
            pltpu.VMEM((2, rows, DIM), jnp.float32),
            pltpu.VMEM((2, rows, 2 * DIM), jnp.bfloat16),
            pltpu.VMEM((DIM, 4 * DIM), jnp.bfloat16),
            pltpu.VMEM((2 * DIM, DIM), jnp.bfloat16),
            pltpu.SemaphoreType.DMA((TAB_BUFS,)),
            pltpu.SemaphoreType.DMA,
            pltpu.SemaphoreType.DMA((PARTS,)),
            pltpu.SemaphoreType.DMA,
        ],
        compiler_params=pltpu.CompilerParams(vmem_limit_bytes=60 * 2**20),
        cost_estimate=pl.CostEstimate(flops=10**9, bytes_accessed=40 * 2**20, transcendentals=0),
        name="unpack",
    )(lengths, buckets, by_place, tiles, centroids)


def score_kernel(
    rows_per, recv_hbm, stored_hbm, out, recv, stored, best, listed, slots, sem, recv_sem, slots_sem
):
    parts = sem.shape[0]
    size = stored.shape[0] // parts

    def copy(i):
        return pltpu.make_async_copy(
            stored_hbm.at[pl.ds(i * size, size)], stored.at[pl.ds(i * size, size)], sem.at[i]
        )

    recv_copy = pltpu.make_async_copy(recv_hbm, recv, recv_sem)
    recv_copy.start()
    for i in range(parts):
        copy(i).start()
    recv_copy.wait()

    def read(src, carry):
        for which in range(2):
            at = pl.multiple_of(src * rows_per + 64 + 16 * which, 16)
            meta = recv[pl.ds(at, 16), :].astype(jnp.float32)
            slot = meta[0:1, :] + 256.0 * meta[8:9, :]
            listed[pl.ds(2 * src + which, 1), :] = slot.astype(jnp.int32)
        return carry

    lax.fori_loop(0, recv.shape[0] // rows_per, read, 0)
    slots_copy = pltpu.make_async_copy(listed, slots, slots_sem)
    slots_copy.start()
    slots_copy.wait()
    for i in range(parts):
        copy(i).wait()

    def one(src, which):
        q = recv[pl.ds(pl.multiple_of(src * rows_per + 32 * which, 16), 32), :]
        zero = jnp.zeros_like(q)
        pair_q = jnp.concatenate(
            [jnp.concatenate([q, zero], axis=1), jnp.concatenate([zero, q], axis=1)], axis=0
        )
        query = 2 * src + which
        sides = [[], []]
        for place in range(16):
            sides[place % 2].append(stored[slots[query, place]])
        both = jnp.concatenate([jnp.concatenate(side, axis=0) for side in sides], axis=1)
        sims = lax.dot_general(
            both, pair_q, (((1,), (1,)), ((), ())), preferred_element_type=jnp.float32
        )
        tops = [
            jnp.max(sims[PTOK * pair : PTOK * (pair + 1), :], axis=0, keepdims=True)
            for pair in range(8)
        ]
        best[pl.ds(query, 1), :] = jnp.concatenate(tops, axis=1)

    def body(src, carry):
        for j in range(SCORE_TURN):
            one(SCORE_TURN * src + j, 0)
            one(SCORE_TURN * src + j, 1)
        return carry

    lax.fori_loop(0, recv.shape[0] // rows_per // SCORE_TURN, body, 0)
    width = best.shape[1]
    member = lax.broadcasted_iota(jnp.int32, (width, 16), 0) // 32
    member = member == lax.broadcasted_iota(jnp.int32, (width, 16), 1)
    out[...] = jnp.dot(
        best[...],
        member.astype(jnp.float32),
        precision=lax.Precision.HIGHEST,
        preferred_element_type=jnp.float32,
    )


def score(rows_per, recv, stored):
    devices = recv.shape[0] // rows_per
    return pl.pallas_call(
        functools.partial(score_kernel, rows_per),
        in_specs=[
            pl.BlockSpec(memory_space=pl.ANY),
            pl.BlockSpec(memory_space=pl.ANY),
        ],
        out_specs=pl.BlockSpec(memory_space=pltpu.VMEM),
        out_shape=jax.ShapeDtypeStruct((2 * devices, 16), jnp.float32),
        scratch_shapes=[
            pltpu.VMEM(recv.shape, jnp.bfloat16),
            pltpu.VMEM((stored.size // (PTOK * DIM), PTOK, DIM), jnp.bfloat16),
            pltpu.VMEM((2 * devices, 16 * 32), jnp.float32),
            pltpu.VMEM((2 * devices, DIM), jnp.int32),
            pltpu.SMEM((2 * devices, DIM), jnp.int32),
            pltpu.SemaphoreType.DMA((16,)),
            pltpu.SemaphoreType.DMA,
            pltpu.SemaphoreType.DMA,
        ],
        compiler_params=pltpu.CompilerParams(vmem_limit_bytes=40 * 2**20),
        cost_estimate=pl.CostEstimate(flops=10**10, bytes_accessed=20 * 2**20, transcendentals=0),
        name="score",
    )(recv, stored.reshape(-1, PTOK, DIM))


def address_kernel(cand, queries, slots, send, dest, seen):
    devices = seen.shape[0]
    q_rows, k_top = cand.shape
    per = slots.shape[1] // k_top
    send[...] = jnp.zeros_like(send)
    for d in range(devices):
        seen[d] = 0
    listed = slots[...]
    low = jnp.bitwise_and(listed, 255).astype(jnp.float32)
    high = jnp.right_shift(listed, 8).astype(jnp.float32)
    in_row = DIM // per
    for t in range(k_top):
        row = t // in_row
        turn = (in_row - t % in_row) * per % DIM
        pieces = [
            pltpu.roll(part[:, row * DIM : (row + 1) * DIM], turn, 1) if turn else part[:, row * DIM : (row + 1) * DIM]
            for part in (low, high)
        ]
        for q in range(q_rows):
            device = cand[q, t]
            place = seen[device]
            seen[device] = 1
            dest[q * k_top + t] = 2 * device + place
            base = pl.multiple_of(device * SEND_ROWS + 32 * place, 16)
            send[pl.ds(base, 32), :] = queries[q]
            meta = [jnp.broadcast_to(piece[q : q + 1, :], (8, DIM)) for piece in pieces]
            at = pl.multiple_of(device * SEND_ROWS + 64 + 16 * place, 16)
            send[pl.ds(at, 16), :] = jnp.concatenate(meta, axis=0).astype(jnp.bfloat16)


def address(cand_dev, queries, cand_slot, devices):
    smem = pl.BlockSpec(memory_space=pltpu.SMEM)
    vmem = pl.BlockSpec(memory_space=pltpu.VMEM)
    return pl.pallas_call(
        address_kernel,
        in_specs=[smem, vmem, vmem],
        out_specs=[vmem, smem],
        out_shape=[
            jax.ShapeDtypeStruct((devices * SEND_ROWS, DIM), jnp.bfloat16),
            jax.ShapeDtypeStruct((cand_dev.size,), jnp.int32),
        ],
        scratch_shapes=[pltpu.SMEM((devices,), jnp.int32)],
        compiler_params=pltpu.CompilerParams(vmem_limit_bytes=24 * 2**20),
        name="address",
    )(cand_dev, queries, cand_slot)


def local(queries, cand_dev, cand_slot, codes, cent_ids, lengths, centroids, buckets):
    devices = lax.axis_size(AXES)
    q_rows, k_top = cand_dev.shape
    per = cand_slot.shape[1] // k_top
    send, dest = address(cand_dev, queries, cand_slot, devices)
    recv = lax.all_to_all(
        send.reshape(devices, SEND_ROWS, DIM), AXES, split_axis=0, concat_axis=0, tiled=True
    )
    stored = unpack(cent_ids, lengths, buckets, codes, centroids)
    scored = score(SEND_ROWS, recv.reshape(devices * SEND_ROWS, DIM), stored)
    returned = lax.all_to_all(
        scored.reshape(devices, 2, per), AXES, split_axis=0, concat_axis=0, tiled=True
    )
    route = jnp.arange(devices * 2, dtype=jnp.int32)[None, :] == dest[:, None]
    result = jnp.dot(
        route.astype(jnp.float32),
        returned.reshape(devices * 2, per),
        precision=lax.Precision.HIGHEST,
        preferred_element_type=jnp.float32,
    )
    return result.reshape(q_rows, k_top * per)


def solution(mesh):
    in_specs = (
        P(AXES, None, None),
        P(AXES, None),
        P(AXES, None),
        P(AXES, None),
        P(AXES, None),
        P(AXES),
        P(),
        P(),
    )
    return jax.shard_map(
        local, mesh=mesh, in_specs=in_specs, out_specs=P(AXES, None), check_vma=False
    )
```
